512 devices in a mesh: ctx: 64 (over y, z), head: 8 (over x, core).
Axes of the slice: x: 4, y: 4, z: 16, core: 2. Of those that a mesh axis runs over, the one named last changes fastest.
Arguments:
- queries: bfloat16 [8192, 64, 576], P('ctx', 'head'), may hold values from -14 to 14
- latents: bfloat16 [8192, 576], P('ctx'), may hold values from -6 to 6
- grad_out: bfloat16 [8192, 64, 512], P('ctx', 'head'), may hold values from -6 to 6
- doc_ids: int32 [8192], replicated, may hold values from 0 to 8191, as said below
Outputs:
- grad_queries: bfloat16 [8192, 64, 576], P('ctx', 'head')
- grad_latents: bfloat16 [8192, 576], P('ctx')
The draws below stay inside these ranges and needn't reach their ends.
Inputs may be any that keep to these rules, and one draw needn't show every extreme that they name: `doc_ids`: each document is a contiguous run of at most 1024 tokens, one has exactly that many, and its label is the position of its first token.
All inputs are finite; a program needn't handle non-finite values.
Results may differ from the reference program's by a relative error of at most 0.0052.
Values may be sent and summed in bfloat16 or wider, within the bound.
A program may use at most 64 MiB of HBM per device.

```python
import jax
import jax.numpy as jnp
from jax import lax

LAT_C = 512
ROPE = 64
HEADS = 64
SPAN = 8
TOK_DEV = 128
LAT = 576
TOKENS = 8192


def joint_draw(key):
    first, second = jax.random.split(jax.random.fold_in(key, 11), 2)
    latents = jnp.clip(jax.random.normal(first, (TOKENS, LAT), jnp.float32), -6.0, 6.0)
    queries = jnp.clip(jax.random.normal(second, (TOKENS, HEADS, LAT), jnp.float32), -6.0, 6.0)
    return (queries, latents)


def draw_queries(key, part):
    return joint_draw(key)[0].astype(jnp.bfloat16)


def draw_latents(key, part):
    return joint_draw(key)[1].astype(jnp.bfloat16)


def draw_doc_ids(key, part):
    key = jax.random.fold_in(key, 5)
    head_key, left_key, right_key = jax.random.split(key, 3)
    longest = SPAN * TOK_DEV
    opening = jax.random.randint(head_key, (1,), 1, TOK_DEV, dtype=jnp.int32)
    left_len = jax.random.randint(left_key, (TOKENS,), 1, longest + 1, dtype=jnp.int32)
    right_len = jax.random.randint(right_key, (TOKENS,), 1, longest + 1, dtype=jnp.int32)
    lengths = jnp.concatenate([opening, jnp.full((1,), longest, jnp.int32), jnp.minimum(left_len, right_len)])
    ends = jnp.cumsum(lengths).astype(jnp.int32)
    positions = jnp.arange(TOKENS, dtype=jnp.int32)
    number = jnp.searchsorted(ends, positions, side='right').astype(jnp.int32)
    starts = jnp.concatenate([jnp.zeros((1,), jnp.int32), ends], axis=0)
    labels = starts[number].astype(jnp.int32)
    return jnp.where(positions == TOKENS - 1, TOKENS - 1, labels).astype(jnp.int32)


def shard_levels(rng, extent, pieces, least, high):
    gain = 1.0
    for dim, parts in pieces:
        steps = jax.random.uniform(jax.random.fold_in(jax.random.fold_in(rng, 6), dim), (parts,), jnp.float32, least / len(pieces), high / len(pieces))
        gain = gain * jnp.repeat(jnp.exp(steps), extent[dim] // parts).reshape((-1,) + (1,) * (len(extent) - 1 - dim))
    return gain


def normal_values(own_key, dims, width, bound, cuts=(), kind=jnp.bfloat16):
    loudness = shard_levels(own_key, dims, cuts, -0.22, 0.18) if cuts else 1.0
    array = jax.random.normal(own_key, dims, jnp.float32) * width * loudness
    return jnp.minimum(jnp.maximum(array, -bound), bound).astype(kind)


def setup_inputs(seed: int = 0) -> dict:
    seeds = jax.random.split(jax.random.key(seed), 5)
    return {
        "queries": draw_queries(jax.random.fold_in(seeds[4], 71), 0),
        "latents": draw_latents(jax.random.fold_in(seeds[4], 71), 0),
        "grad_out": normal_values(seeds[2], (TOKENS, HEADS, LAT_C), 1.0, 6.0, ((0, 64), (1, 8))),
        "doc_ids": draw_doc_ids(jax.random.fold_in(seeds[4], 71), 0),
    }


score_scale = 192.0 ** -0.5


def attend_backward(query_rows, grad_rows, key_rows, visible):
    query_f = query_rows.astype(jnp.float32)
    grad_f = grad_rows.astype(jnp.float32)
    key_f = key_rows.astype(jnp.float32)
    value_f = key_f[:, :LAT_C]
    scores = jnp.einsum("thc,kc->htk", query_f, key_f) * score_scale
    scores = jnp.where(visible[None], scores, -1e30)
    row_max = jnp.max(scores, axis=-1, keepdims=True)
    expo = jnp.where(visible[None], jnp.exp(scores - row_max), 0.0)
    weights = expo / jnp.sum(expo, axis=-1, keepdims=True)
    probs = weights.astype(jnp.bfloat16)
    probs_f = probs.astype(jnp.float32)
    output = jnp.einsum("htk,kc->thc", probs_f, value_f)
    delta = jnp.sum(grad_f * output, axis=-1)
    grad_probs = jnp.einsum("thc,kc->htk", grad_f, value_f)
    grad_scores = (weights * (grad_probs - jnp.transpose(delta)[:, :, None]) * score_scale).astype(jnp.bfloat16)
    grad_scores_f = grad_scores.astype(jnp.float32)
    grad_query = jnp.einsum("htk,kc->thc", grad_scores_f, key_f).astype(jnp.bfloat16)
    grad_keys = jnp.einsum("htk,thc->kc", grad_scores_f, query_f)
    grad_values = jnp.einsum("htk,thc->kc", probs_f, grad_f)
    grad_keys = grad_keys + jnp.pad(grad_values, ((0, 0), (0, ROPE)))
    return grad_query, grad_keys


def reference(queries, latents, grad_out, doc_ids):
    block = TOK_DEV
    window = (SPAN + 1) * block
    lead = SPAN * block
    padded_lat = jnp.concatenate([jnp.zeros((lead, LAT), latents.dtype), latents], axis=0)
    padded_ids = jnp.concatenate([jnp.full((lead,), -1, jnp.int32), doc_ids.astype(jnp.int32)], axis=0)
    blocks_total = TOKENS // block

    def one_block(carry, number):
        start = (number * block).astype(jnp.int32)
        query_rows = lax.dynamic_slice_in_dim(queries, start, block, 0)
        grad_rows = lax.dynamic_slice_in_dim(grad_out, start, block, 0)
        key_rows = lax.dynamic_slice_in_dim(padded_lat, start, window, 0)
        key_ids = lax.dynamic_slice_in_dim(padded_ids, start, window, 0)
        query_ids = lax.dynamic_slice_in_dim(doc_ids.astype(jnp.int32), start, block, 0)
        query_pos = start + jnp.arange(block, dtype=jnp.int32)
        key_pos = start - lead + jnp.arange(window, dtype=jnp.int32)
        visible = (key_ids[None, :] == query_ids[:, None]) & (key_pos[None, :] <= query_pos[:, None])
        grad_query, grad_keys = attend_backward(query_rows, grad_rows, key_rows, visible)
        current = lax.dynamic_slice_in_dim(carry, start, window, 0)
        carry = lax.dynamic_update_slice_in_dim(carry, current + grad_keys, start, 0)
        return carry, grad_query

    init = jnp.zeros((lead + TOKENS, LAT), jnp.float32)
    totals, grad_blocks = lax.scan(one_block, init, jnp.arange(blocks_total, dtype=jnp.int32))
    grad_queries = grad_blocks.reshape(TOKENS, HEADS, LAT)
    grad_latents = totals[lead:].astype(jnp.bfloat16)
    return grad_queries, grad_latents
```

```python
import functools

import jax
import jax.numpy as jnp
from jax import lax
from jax.experimental import pallas as pl
from jax.experimental.pallas import tpu as pltpu
from jax.sharding import PartitionSpec as P

LAT_C = 512
SPAN = 8
LANES = 256

score_scale = 192.0 ** (-0.5)
exp2_scale = score_scale * 1.4426950408889634
HIDDEN = -1e30
MESH = pl.DeviceIdType.MESH
NT = (((1,), (1,)), ((), ()))
TN = (((0,), (0,)), ((), ()))


def schedule(span):
    order = []
    for k in range(span, -1, -2):
        order.append(("D", k))
        order.append(("A", k))
        if k > 0:
            order.append(("A", k - 1))
        if k + 2 <= span:
            order.append(("B", k + 2))
            order.append(("B", k + 1))
        if k + 4 <= span:
            order.append(("C", span - (span - k - 4) // 2))
    last = span % 2
    order.append(("B", last))
    if last == 1:
        order.append(("B", 0))
    done = [k for op, k in order if op == "C"]
    rest = [k for k in range(span, -1, -1) if k not in done]
    for n, k in enumerate(rest):
        order.append(("C", k))
        order.append(("Q", n))
    return order


def kernel(
    span, nctx, nhead,
    doc_ref, q_hbm, g_hbm, lat_hbm, gq_hbm, gl_hbm,
    kwin, q, g, ew, gp, pw, ds, starts, tops, part, csend, crecv, xsend, xrecv, zsend, zrecv, gqbuf, glbuf,
    local, gz_s, gz_r, gx_s, gx_r, gc_s, gc_r, rc_s, rc_r, rx_s, rx_r, rz_s, rz_r, ag_s, ag_r,
):
    tok = lat_hbm.shape[0]
    rows = q_hbm.shape[0]
    heads = rows // tok
    half, piece, nx = tok // 2, tok // nhead, nhead // 2
    chunks = rows // LANES
    s = lax.axis_index("ctx")
    hd = lax.axis_index("head")
    x, c = hd // 2, lax.rem(hd, 2)
    right, left = lax.rem(s + 1, nctx), lax.rem(s + nctx - 1, nctx)
    mine = c * half + x * piece

    def xpeer(j):
        return lax.rem(x + j, nx)

    loads = [
        pltpu.make_async_copy(lat_hbm, kwin.at[pl.ds(0, tok)], local.at[0]),
        pltpu.make_async_copy(q_hbm, q, local.at[1]),
        pltpu.make_async_copy(g_hbm, g, local.at[2]),
    ]
    for load in loads:
        load.start()

    barrier = pltpu.get_barrier_semaphore()
    peers = [(right, hd), (left, hd)] + [(s, lax.rem(hd + j, nhead)) for j in range(1, nhead)]
    for peer in peers:
        pl.semaphore_signal(barrier, inc=1, device_id=peer, device_id_type=MESH)
    pl.semaphore_wait(barrier, len(peers))

    def remote(src, dst, send, recv, dev):
        return pltpu.make_async_remote_copy(
            src_ref=src, dst_ref=dst, send_sem=send, recv_sem=recv, device_id=dev, device_id_type=MESH
        )

    def rows_at(block, start, count):
        return pl.ds(pl.multiple_of(block * tok + start, 16), count)

    sent = []

    def go(copy):
        copy.start()
        sent.append(copy)

    def g_z(k):
        src = lat_hbm.at[rows_at(0, mine, piece)] if k == 1 else kwin.at[rows_at(k - 1, mine, piece)]
        return remote(src, kwin.at[rows_at(k, mine, piece)], gz_s.at[k - 1], gz_r.at[k - 1], (right, hd))

    def g_x(k, j):
        ref = kwin.at[rows_at(k, mine, piece)]
        return remote(ref, ref, gx_s.at[(k - 1) * (nx - 1) + j - 1], gx_r.at[(k - 1) * (nx - 1) + j - 1], (s, xpeer(j) * 2 + c))

    def g_c(k):
        ref = kwin.at[rows_at(k, c * half, half)]
        return remote(ref, ref, gc_s.at[k - 1], gc_r.at[k - 1], (s, x * 2 + 1 - c))

    go(g_z(1))

    doc = doc_ref[pl.ds(s, 1), :] - (s - span) * tok
    halves = lax.broadcasted_iota(jnp.int32, (16, tok), 0) == 0
    coded = jnp.where(halves, lax.shift_right_arithmetic(doc, 5), doc & 31).astype(jnp.float32).astype(jnp.bfloat16)
    spread = (
        lax.shift_right_logical(lax.broadcasted_iota(jnp.int32, (tok, rows), 1), heads.bit_length() - 1)
        == lax.broadcasted_iota(jnp.int32, (tok, rows), 0)
    )
    spread = jnp.where(spread, 1.0, 0.0).astype(jnp.bfloat16)
    coded = jnp.dot(coded, spread, preferred_element_type=jnp.float32)
    starts[...] = coded[0:1, :] * 32.0 + coded[1:2, :]

    for load in loads:
        load.wait()

    def scores(k):
        def chunk(n, _):
            at = pl.ds(pl.multiple_of(n * LANES, LANES), LANES)
            here = pl.ds(k * tok, tok)
            score = lax.dot_general(kwin[here, :], q[at, :], NT, preferred_element_type=jnp.float32)
            grad = lax.dot_general(kwin[here, :LAT_C], g[at, :], NT, preferred_element_type=jnp.float32)
            row = lax.broadcasted_iota(jnp.int32, (tok, LANES), 0)
            seen = (row + (span - k) * tok).astype(jnp.float32) >= starts[:, at]
            if k == 0:
                lane = lax.broadcasted_iota(jnp.int32, (tok, LANES), 1) + n * LANES
                seen = seen & (row <= lax.shift_right_logical(lane, heads.bit_length() - 1))
            score = jnp.where(seen, score, HIDDEN)
            top = jnp.max(score, axis=0, keepdims=True)
            if k > 0:
                before = tops[k - 1 : k, at]
                top = jnp.maximum(top, before)
            expo = jnp.exp2((score - top) * exp2_scale)
            total = jnp.sum(expo, axis=0, keepdims=True)
            if k > 0:
                total = total + tops[span + 1 : span + 2, at] * jnp.exp2((before - top) * exp2_scale)
            tops[k : k + 1, at] = top
            tops[span + 1 : span + 2, at] = total
            ew[here, at] = expo
            gp[here, at] = grad
            return 0

        lax.fori_loop(0, chunks, chunk, 0)

    scores(0)
    for t in range(1, span + 3):
        if t <= span:
            g_z(t).wait_recv()
            if t < span:
                go(g_z(t + 1))
            for j in range(1, nx):
                go(g_x(t, j))
        if 2 <= t <= span + 1:
            for j in range(1, nx):
                g_x(t - 1, j).wait_recv()
            go(g_c(t - 1))
        if t >= 3:
            g_c(t - 2).wait_recv()
            scores(t - 2)

    def soften(n, _):
        at = pl.ds(pl.multiple_of(n * LANES, LANES), LANES)
        over = 1.0 / tops[span + 1 : span + 2, at]
        final = tops[span : span + 1, at]
        delta = jnp.zeros((1, LANES), jnp.float32)
        for k in range(span + 1):
            here = pl.ds(k * tok, tok)
            weight = ew[here, at] * (jnp.exp2((tops[k : k + 1, at] - final) * exp2_scale) * over)
            prob = weight.astype(jnp.bfloat16)
            pw[here, at] = prob
            ew[here, at] = weight
            delta = delta + jnp.sum(prob.astype(jnp.float32) * gp[here, at], axis=0, keepdims=True)
        for k in range(span + 1):
            here = pl.ds(k * tok, tok)
            ds[here, at] = (ew[here, at] * (gp[here, at] - delta) * score_scale).astype(jnp.bfloat16)
        return 0

    lax.fori_loop(0, chunks, soften, 0)

    def products(k):
        low = max(k - 1, 0)
        here = pl.ds(low * tok, (k + 1 - low) * tok)
        part[here, :] = jnp.dot(ds[here, :], q[...], preferred_element_type=jnp.float32)
        part[here, :LAT_C] += jnp.dot(pw[here, :], g[...], preferred_element_type=jnp.float32)

    def r_c(k):
        at = pl.ds(k * half, half)
        return remote(csend.at[at], crecv.at[at], rc_s.at[k], rc_r.at[k], (s, x * 2 + 1 - c))

    def r_x(k, j):
        src = xsend.at[pl.ds(pl.multiple_of(k * half + xpeer(j) * piece, 16), piece)]
        dst = xrecv.at[pl.ds((k * (nx - 1) + j - 1) * piece, piece)]
        return remote(src, dst, rx_s.at[k * (nx - 1) + j - 1], rx_r.at[k * (nx - 1) + j - 1], (s, xpeer(j) * 2 + c))

    def r_z(k):
        at = pl.ds((k - 1) * piece, piece)
        return remote(zsend.at[at], zrecv.at[at], rz_s.at[k - 1], rz_r.at[k - 1], (left, hd))

    outs = []

    def ag(j):
        ref = glbuf.at[rows_at(0, mine, piece)]
        return remote(ref, ref, ag_s.at[j - 1], ag_r.at[j - 1], (s, lax.rem(hd + j, nhead)))

    for op, k in schedule(span):
        if op == "D":
            products(k)
        elif op == "A":
            csend[pl.ds(k * half, half), :] = part[rows_at(k, (1 - c) * half, half), :].astype(jnp.bfloat16)
            go(r_c(k))
        elif op == "B":
            r_c(k).wait_recv()
            total = part[rows_at(k, c * half, half), :] + crecv[pl.ds(k * half, half), :].astype(jnp.float32)
            part[rows_at(k, c * half, half), :] = total
            xsend[pl.ds(k * half, half), :] = total.astype(jnp.bfloat16)
            for j in range(1, nx):
                go(r_x(k, j))
        elif op == "C":
            total = part[rows_at(k, mine, piece), :]
            for j in range(1, nx):
                r_x(k, j).wait_recv()
                total = total + xrecv[pl.ds((k * (nx - 1) + j - 1) * piece, piece), :].astype(jnp.float32)
            if k < span:
                r_z(k + 1).wait_recv()
                total = total + zrecv[pl.ds(k * piece, piece), :].astype(jnp.float32)
            if k > 0:
                zsend[pl.ds((k - 1) * piece, piece), :] = total.astype(zsend.dtype)
                go(r_z(k))
            else:
                glbuf[rows_at(0, mine, piece), :] = total.astype(jnp.bfloat16)
                for j in range(1, nhead):
                    go(ag(j))
        elif k < chunks:
            at = pl.ds(k * LANES, LANES)
            gqbuf[at, :] = lax.dot_general(ds[:, at], kwin[...], TN, preferred_element_type=jnp.float32).astype(jnp.bfloat16)
            out = pltpu.make_async_copy(gqbuf.at[at], gq_hbm.at[at], local.at[3 + k])
            out.start()
            outs.append(out)

    for j in range(1, nhead):
        ag(j).wait_recv()
    last = pltpu.make_async_copy(glbuf, gl_hbm, local.at[0])
    last.start()
    for copy in sent:
        copy.wait_send()
    for out in outs:
        out.wait()
    last.wait()


def on_device(nctx, nhead, span, queries, latents, grad_out, doc_ids):
    tok, heads, lat = queries.shape
    rows = tok * heads
    window = (span + 1) * tok
    piece, nx = tok // nhead, nhead // 2
    bf16, f32 = jnp.bfloat16, jnp.float32
    dma = pltpu.SemaphoreType.DMA
    grad_queries, grad_latents = pl.pallas_call(
        functools.partial(kernel, span, nctx, nhead),
        out_shape=(
            jax.ShapeDtypeStruct((rows, lat), bf16),
            jax.ShapeDtypeStruct((tok, lat), bf16),
        ),
        in_specs=[pl.BlockSpec(memory_space=pltpu.VMEM)] + [pl.BlockSpec(memory_space=pl.ANY)] * 3,
        out_specs=(pl.BlockSpec(memory_space=pl.ANY), pl.BlockSpec(memory_space=pl.ANY)),
        scratch_shapes=[
            pltpu.VMEM((window, lat), bf16),
            pltpu.VMEM((rows, lat), bf16),
            pltpu.VMEM((rows, LAT_C), bf16),
            pltpu.VMEM((window, rows), f32),
            pltpu.VMEM((window, rows), f32),
            pltpu.VMEM((window, rows), bf16),
            pltpu.VMEM((window, rows), bf16),
            pltpu.VMEM((1, rows), f32),
            pltpu.VMEM((span + 2, rows), f32),
            pltpu.VMEM((window, lat), f32),
            pltpu.VMEM(((span + 1) * tok // 2, lat), bf16),
            pltpu.VMEM(((span + 1) * tok // 2, lat), bf16),
            pltpu.VMEM(((span + 1) * tok // 2, lat), bf16),
            pltpu.VMEM(((span + 1) * (nx - 1) * piece, lat), bf16),
            pltpu.VMEM((span * piece, lat), f32),
            pltpu.VMEM((span * piece, lat), f32),
            pltpu.VMEM((rows, lat), bf16),
            pltpu.VMEM((tok, lat), bf16),
            dma((3 + rows // LANES,)),
            dma((span,)), dma((span,)),
            dma((span * (nx - 1),)), dma((span * (nx - 1),)),
            dma((span,)), dma((span,)),
            dma((span + 1,)), dma((span + 1,)),
            dma(((span + 1) * (nx - 1),)), dma(((span + 1) * (nx - 1),)),
            dma((span,)), dma((span,)),
            dma((nhead - 1,)), dma((nhead - 1,)),
        ],
        compiler_params=pltpu.CompilerParams(
            collective_id=0, has_side_effects=True, vmem_limit_bytes=48 * 1024 * 1024
        ),
    )(doc_ids.reshape(nctx, tok), queries.reshape(rows, lat), grad_out.reshape(rows, LAT_C), latents)
    return grad_queries.reshape(queries.shape), grad_latents


def solution(mesh):
    nctx, nhead = mesh.shape["ctx"], mesh.shape["head"]
    placed = (P("ctx", "head", None), P("ctx", None), P("ctx", "head", None), P())
    return jax.shard_map(
        functools.partial(on_device, nctx, nhead, SPAN),
        mesh=mesh,
        in_specs=placed,
        out_specs=(P("ctx", "head", None), P("ctx", None)),
        check_vma=False,
    )
```

```python
import functools

import jax
import jax.numpy as jnp
from jax import lax
from jax.experimental import pallas as pl
from jax.experimental.pallas import tpu as pltpu
from jax.sharding import PartitionSpec as P

LAT_C = 512
SPAN = 8
LANES = 128
SC_HEADS = 4
SOFT_HEADS = 2
Q_HEADS = 2

score_scale = 192.0 ** (-0.5)
exp2_scale = score_scale * 1.4426950408889634
HIDDEN = -1e30
MESH = pl.DeviceIdType.MESH
NT = (((1,), (1,)), ((), ()))

STRAIGHT = (6, 3, 2, 1)
RELAYED = {3: (5, 4), 6: (8, 7)}
GROUPS = ((1, 2), (3, 1), (6, 1), (4, 2), (7, 2))
BACK = ((7, 2), (4, 2), (6, 1), (3, 1), (1, 2), (0, 1))


def kernel(
    span, nctx, nhead,
    doc_ref, q_hbm, g_hbm, lat_hbm, gq_hbm, gl_hbm,
    kwin, kt, q, graw, gf, g, ew, gp, pw, ds, tops, part, csend, crecv, xsend, xrecv, zsend, zrecv, gqbuf, glbuf,
    local, gz_s, gz_r, gx_s, gx_r, gc_s, gc_r, rc_s, rc_r, rx_s, rx_r, rz_s, rz_r, ag_s, ag_r,
):
    heads, lat, tok = q_hbm.shape
    rows = heads * tok
    half, piece, nx = tok // 2, tok // nhead, nhead // 2
    s = lax.axis_index("ctx")
    hd = lax.axis_index("head")
    x, c = hd // 2, lax.rem(hd, 2)
    mine = pl.multiple_of(c * half + x * piece, 16)

    def xpeer(j):
        return lax.rem(x + j, nx)

    def ctx(step):
        return lax.rem(s + step + nctx, nctx)

    barrier = pltpu.get_barrier_semaphore()
    peers = [(s, lax.rem(hd + j, nhead)) for j in range(1, nhead)]
    for step in STRAIGHT:
        peers += [(ctx(step), hd), (ctx(-step), hd)]
    for peer in peers:
        pl.semaphore_signal(barrier, inc=1, device_id=peer, device_id_type=MESH)

    loads = [pltpu.make_async_copy(lat_hbm, kt.at[:, pl.ds(0, tok)], local.at[0])]
    loads += [pltpu.make_async_copy(g_hbm, graw, local.at[1])]
    loads += [pltpu.make_async_copy(q_hbm.at[h], q.at[:, pl.ds(h * tok, tok)], local.at[2 + h]) for h in range(heads)]
    for load in loads:
        load.start()

    def remote(src, dst, send, recv, dev):
        return pltpu.make_async_remote_copy(
            src_ref=src, dst_ref=dst, send_sem=send, recv_sem=recv, device_id=dev, device_id_type=MESH
        )

    sent = []

    def go(copy):
        copy.start()
        sent.append(copy)

    def g_z(k, step):
        src = kwin.at[k - step, pl.ds(mine, piece)]
        return remote(src, kwin.at[k, pl.ds(mine, piece)], gz_s.at[k - 1], gz_r.at[k - 1], (ctx(step), hd))

    def g_x(n, j):
        ref = kwin.at[pl.ds(*GROUPS[n]), pl.ds(mine, piece)]
        at = n * (nx - 1) + j - 1
        return remote(ref, ref, gx_s.at[at], gx_r.at[at], (s, xpeer(j) * 2 + c))

    def g_c(n):
        ref = kwin.at[pl.ds(*GROUPS[n]), pl.ds(pl.multiple_of(c * half, 16), half)]
        return remote(ref, ref, gc_s.at[n], gc_r.at[n], (s, x * 2 + 1 - c))

    start = doc_ref[pl.ds(s, 1), :] - (s - span) * tok

    def scores(k, count):
        height = count * tok
        width = SC_HEADS * tok
        starts = jnp.concatenate([start] * SC_HEADS, axis=1)
        keys = kwin[k : k + count].reshape(height, lat)
        row = lax.broadcasted_iota(jnp.int32, (height, width), 0)
        place = row + (span - k) * tok
        if count == 2:
            place = jnp.where(row < tok, place, place - 2 * tok)
        seen = place >= starts
        if k == 0:
            token = lax.broadcasted_iota(jnp.int32, (height, tok), 1)
            seen = seen & (row <= jnp.concatenate([token] * SC_HEADS, axis=1))
        here = pl.ds(k * tok, height)

        def chunk(n, _):
            at = pl.ds(pl.multiple_of(n * width, width), width)
            score = jnp.dot(keys, q[:, at], preferred_element_type=jnp.float32)
            grad = lax.dot_general(keys[:, :LAT_C], g[at, :], NT, preferred_element_type=jnp.float32)
            score = jnp.where(seen, score, HIDDEN)
            top = jnp.max(score, axis=0, keepdims=True)
            if k > 0:
                before = tops[span + 2 : span + 3, at]
                top = jnp.maximum(top, before)
            expo = jnp.exp2((score - top) * exp2_scale)
            total = jnp.sum(expo, axis=0, keepdims=True)
            if k > 0:
                total = total + tops[span + 1 : span + 2, at] * jnp.exp2((before - top) * exp2_scale)
            for extra in range(count):
                tops[k + extra : k + extra + 1, at] = top
            tops[span + 1 : span + 2, at] = total
            tops[span + 2 : span + 3, at] = top
            ew[here, at] = expo
            gp[here, at] = grad
            return 0

        lax.fori_loop(0, heads // SC_HEADS, chunk, 0)

    def turn(k):
        kt[:, pl.ds(k * tok, tok)] = kwin[k].T

    loads[0].wait()
    kwin[0] = kt[:, pl.ds(0, tok)].T
    loads[1].wait()
    for n in range(LAT_C // LANES):
        at = pl.ds(n * LANES, LANES)
        gf[n] = graw[:, at].astype(jnp.float32)
        for h in range(heads):
            g[pl.ds(h * tok, tok), at] = gf[n, pl.ds(h, tok, stride=heads), :].astype(jnp.bfloat16)
    for load in loads[2:]:
        load.wait()
    scores(0, 1)

    pl.semaphore_wait(barrier, len(peers))

    for k in STRAIGHT:
        go(g_z(k, k))

    def spread(n):
        for j in range(1, nx):
            go(g_x(n, j))

    def across(n):
        for j in range(1, nx):
            g_x(n, j).wait_recv()
        go(g_c(n))

    def take(n):
        g_c(n).wait_recv()
        k, count = GROUPS[n]
        scores(k, count)
        for extra in range(count):
            turn(k + extra)

    def relay(k):
        g_z(k, k).wait_recv()
        for later in RELAYED[k]:
            go(g_z(later, later - k))

    relay(3)
    g_z(1, 1).wait_recv()
    g_z(2, 2).wait_recv()
    spread(0)
    spread(1)
    relay(6)
    spread(2)
    across(0)
    across(1)
    g_z(4, 1).wait_recv()
    g_z(5, 2).wait_recv()
    spread(3)
    across(2)
    take(0)
    g_z(7, 1).wait_recv()
    g_z(8, 2).wait_recv()
    spread(4)
    take(1)
    across(3)
    take(2)
    across(4)
    take(3)
    take(4)

    def soften(n, _):
        width = SOFT_HEADS * tok
        at = pl.ds(pl.multiple_of(n * width, width), width)
        over = 1.0 / tops[span + 1 : span + 2, at]
        final = tops[span + 2 : span + 3, at]
        delta = jnp.zeros((1, width), jnp.float32)
        for k in range(span + 1):
            here = pl.ds(k * tok, tok)
            weight = ew[here, at] * (jnp.exp2((tops[k : k + 1, at] - final) * exp2_scale) * over)
            prob = weight.astype(jnp.bfloat16)
            pw[here, at] = prob
            ew[here, at] = weight
            delta = delta + jnp.sum(prob.astype(jnp.float32) * gp[here, at], axis=0, keepdims=True)
        for k in range(span + 1):
            here = pl.ds(k * tok, tok)
            ds[here, at] = (ew[here, at] * (gp[here, at] - delta) * score_scale).astype(jnp.bfloat16)
        return 0

    lax.fori_loop(0, heads // SOFT_HEADS, soften, 0)

    def r_c(n):
        at = pl.ds(*BACK[n])
        return remote(csend.at[at], crecv.at[at], rc_s.at[n], rc_r.at[n], (s, x * 2 + 1 - c))

    def r_x(n, j):
        src = xsend.at[pl.ds(*BACK[n]), pl.ds(pl.multiple_of(xpeer(j) * piece, 16), piece)]
        dst = xrecv.at[j - 1, pl.ds(*BACK[n])]
        at = n * (nx - 1) + j - 1
        return remote(src, dst, rx_s.at[at], rx_r.at[at], (s, xpeer(j) * 2 + c))

    def r_z(k, step):
        return remote(zsend.at[k - 1], zrecv.at[k - 1], rz_s.at[k - 1], rz_r.at[k - 1], (ctx(-step), hd))

    def products(n):
        k, count = BACK[n]
        here = pl.ds(k * tok, count * tok)
        low, high = pl.multiple_of(c * half, 16), pl.multiple_of((1 - c) * half, 16)
        part[here, :] = lax.dot_general(ds[here, :], q[...], NT, preferred_element_type=jnp.float32)
        part[here, :LAT_C] += jnp.dot(pw[here, :], g[...], preferred_element_type=jnp.float32)
        for e in range(k, k + count):
            csend[e] = part[pl.ds(pl.multiple_of(e * tok + high, 16), half), :].astype(jnp.bfloat16)
        go(r_c(n))

    def pair(n):
        r_c(n).wait_recv()
        k, count = BACK[n]
        for e in range(k, k + count):
            at = pl.ds(pl.multiple_of(e * tok + c * half, 16), half)
            total = part[at, :] + crecv[e].astype(jnp.float32)
            part[at, :] = total
            xsend[e] = total.astype(jnp.bfloat16)
        for j in range(1, nx):
            go(r_x(n, j))

    def chips(n):
        for j in range(1, nx):
            r_x(n, j).wait_recv()

    def mine_of(k):
        total = part[pl.ds(pl.multiple_of(k * tok + mine, 16), piece), :]
        for j in range(1, nx):
            total = total + xrecv[j - 1, k].astype(jnp.float32)
        return total

    def leaf(k, step):
        zsend[k - 1] = mine_of(k).astype(jnp.bfloat16)
        go(r_z(k, step))

    def node(k):
        total = mine_of(k)
        for later in RELAYED[k]:
            r_z(later, later - k).wait_recv()
            total = total + zrecv[later - 1].astype(jnp.float32)
        zsend[k - 1] = total.astype(jnp.bfloat16)
        go(r_z(k, k))

    outs = []

    def queries(n):
        width = Q_HEADS * tok
        at = pl.ds(n * width, width)
        gqbuf[:, at] = jnp.dot(kt[...], ds[:, at], preferred_element_type=jnp.float32).astype(jnp.bfloat16)
        for h in range(n * Q_HEADS, (n + 1) * Q_HEADS):
            out = pltpu.make_async_copy(gqbuf.at[:, pl.ds(h * tok, tok)], gq_hbm.at[h], local.at[2 + h])
            out.start()
            outs.append(out)

    def ag(j):
        ref = glbuf.at[pl.ds(mine, piece)]
        return remote(ref, ref, ag_s.at[j - 1], ag_r.at[j - 1], (s, lax.rem(hd + j, nhead)))

    products(0)
    products(1)
    pair(0)
    products(2)
    pair(1)
    products(3)
    pair(2)
    products(4)
    pair(3)
    products(5)
    chips(0)
    leaf(8, 2)
    leaf(7, 1)
    pair(4)
    chips(1)
    leaf(5, 2)
    leaf(4, 1)
    pair(5)
    queries(0)
    chips(2)
    node(6)
    chips(3)
    node(3)
    chips(4)
    leaf(2, 2)
    leaf(1, 1)
    queries(1)
    queries(2)
    queries(3)
    chips(5)
    total = mine_of(0)
    for k in reversed(STRAIGHT):
        r_z(k, k).wait_recv()
        total = total + zrecv[k - 1].astype(jnp.float32)
    glbuf[pl.ds(mine, piece), :] = total.astype(jnp.bfloat16)
    for j in range(1, nhead):
        go(ag(j))
    for out in outs:
        out.wait()
    for j in range(1, nhead):
        ag(j).wait_recv()
    last = pltpu.make_async_copy(glbuf, gl_hbm, local.at[0])
    last.start()
    for copy in sent:
        copy.wait_send()
    last.wait()


def on_device(nctx, nhead, span, queries, latents, grad_out, doc_ids):
    tok, heads, lat = queries.shape
    rows = tok * heads
    window = (span + 1) * tok
    piece, nx = tok // nhead, nhead // 2
    bf16, f32 = jnp.bfloat16, jnp.float32
    dma = pltpu.SemaphoreType.DMA
    groups, back = len(GROUPS), len(BACK)
    grad_queries, grad_latents = pl.pallas_call(
        functools.partial(kernel, span, nctx, nhead),
        out_shape=(
            jax.ShapeDtypeStruct((heads, lat, tok), bf16),
            jax.ShapeDtypeStruct((tok, lat), bf16),
        ),
        in_specs=[pl.BlockSpec(memory_space=pltpu.VMEM)] + [pl.BlockSpec(memory_space=pltpu.HBM)] * 3,
        out_specs=(pl.BlockSpec(memory_space=pltpu.HBM), pl.BlockSpec(memory_space=pl.ANY)),
        scratch_shapes=[
            pltpu.VMEM((span + 1, tok, lat), bf16),
            pltpu.VMEM((lat, window), bf16),
            pltpu.VMEM((lat, rows), bf16),
            pltpu.VMEM((rows, LAT_C), bf16),
            pltpu.VMEM((LAT_C // LANES, rows, LANES), f32),
            pltpu.VMEM((rows, LAT_C), bf16),
            pltpu.VMEM((window, rows), f32),
            pltpu.VMEM((window, rows), f32),
            pltpu.VMEM((window, rows), bf16),
            pltpu.VMEM((window, rows), bf16),
            pltpu.VMEM((span + 3, rows), f32),
            pltpu.VMEM((window, lat), f32),
            pltpu.VMEM((span + 1, tok // 2, lat), bf16),
            pltpu.VMEM((span + 1, tok // 2, lat), bf16),
            pltpu.VMEM((span + 1, tok // 2, lat), bf16),
            pltpu.VMEM((nx - 1, span + 1, piece, lat), bf16),
            pltpu.VMEM((span, piece, lat), bf16),
            pltpu.VMEM((span, piece, lat), bf16),
            pltpu.VMEM((lat, rows), bf16),
            pltpu.VMEM((tok, lat), bf16),
            dma((2 + heads,)),
            dma((span,)), dma((span,)),
            dma((groups * (nx - 1),)), dma((groups * (nx - 1),)),
            dma((groups,)), dma((groups,)),
            dma((back,)), dma((back,)),
            dma((back * (nx - 1),)), dma((back * (nx - 1),)),
            dma((span,)), dma((span,)),
            dma((nhead - 1,)), dma((nhead - 1,)),
        ],
        compiler_params=pltpu.CompilerParams(
            collective_id=0, has_side_effects=True, vmem_limit_bytes=56 * 1024 * 1024
        ),
    )(doc_ids.reshape(nctx, tok), queries.transpose(1, 2, 0), grad_out.reshape(rows, LAT_C), latents.T)
    return grad_queries.transpose(2, 0, 1), grad_latents


def solution(mesh):
    nctx, nhead = mesh.shape["ctx"], mesh.shape["head"]
    placed = (P("ctx", "head", None), P("ctx", None), P("ctx", "head", None), P())
    return jax.shard_map(
        functools.partial(on_device, nctx, nhead, SPAN),
        mesh=mesh,
        in_specs=placed,
        out_specs=(P("ctx", "head", None), P("ctx", None)),
        check_vma=False,
    )
```

```python
import functools

import jax
import jax.numpy as jnp
from jax import lax
from jax.experimental import pallas as pl
from jax.experimental.pallas import tpu as pltpu
from jax.sharding import PartitionSpec as P

LAT_C = 512
SPAN = 8
LANES = 128
SC_HEADS = 4
SOFT_HEADS = 2
Q_HEADS = 2

score_scale = 192.0 ** (-0.5)
exp2_scale = score_scale * 1.4426950408889634
HIDDEN = -1e30
MESH = pl.DeviceIdType.MESH
NT = (((1,), (1,)), ((), ()))

STRAIGHT = (6, 3, 2, 1)
FROM = {1: 1, 2: 2, 3: 3, 6: 6, 4: 1, 5: 2, 7: 1, 8: 2}
FIRST = (6, 3, 2, 1)
DIRECT = ()
GATHER = (
    ("arrive", 3), ("arrive", 1), ("arrive", 2), ("spread", 0), ("spread", 1), ("arrive", 6), ("spread", 2), ("across", 0),
    ("across", 1), ("arrive", 4), ("arrive", 5), ("spread", 3), ("across", 2), ("take", 0), ("arrive", 7), ("arrive", 8),
    ("spread", 4), ("take", 1), ("across", 3), ("take", 2), ("across", 4), ("take", 3), ("take", 4),
)
RELAYED = {3: (5, 4), 6: (8, 7)}
GROUPS = ((1, 2), (3, 1), (6, 1), (4, 2), (7, 2))
BACK = ((7, 2), (4, 2), (6, 1), (3, 1), (1, 2), (0, 1))
RETURN = (
    ("products", 0), ("products", 1), ("pair", 0), ("products", 2), ("pair", 1), ("products", 3), ("pair", 2),
    ("products", 4), ("chips", 0), ("leaves", 7), ("pair", 3), ("products", 5), ("pair", 4), ("chips", 1), ("leaves", 4),
    ("pair", 5), ("chips", 2), ("node", 6), ("chips", 3), ("node", 3), ("chips", 4), ("leaves", 1),
    ("queries", 0), ("queries", 1), ("queries", 2), ("queries", 3), ("chips", 5),
)


def kernel(
    span, nctx, nhead,
    doc_ref, q_hbm, g_hbm, lat_hbm, gq_hbm, gl_hbm,
    kwin, kt, q, graw, gf, g, ew, gp, pw, ds, tops, part, csend, crecv, xsend, xrecv, zsend, zrecv, gqbuf, glbuf, glturn,
    local, gz_s, gz_r, gx_s, gx_r, gc_s, gc_r, rc_s, rc_r, rx_s, rx_r, rz_s, rz_r, ag_s, ag_r,
):
    heads, lat, tok = q_hbm.shape
    rows = heads * tok
    half, piece, nx = tok // 2, tok // nhead, nhead // 2
    s = lax.axis_index("ctx")
    hd = lax.axis_index("head")
    x, c = hd // 2, lax.rem(hd, 2)
    mine = pl.multiple_of(c * half + x * piece, 16)

    def xpeer(j):
        return lax.rem(x + j, nx)

    def ctx(step):
        return lax.rem(s + step + nctx, nctx)

    barrier = pltpu.get_barrier_semaphore()
    peers = [(s, lax.rem(hd + j, nhead)) for j in range(1, nhead)]
    for step in STRAIGHT:
        peers += [(ctx(step), hd), (ctx(-step), hd)]
    for peer in peers:
        pl.semaphore_signal(barrier, inc=1, device_id=peer, device_id_type=MESH)

    loads = [pltpu.make_async_copy(lat_hbm, kt.at[:, pl.ds(0, tok)], local.at[0])]
    loads += [pltpu.make_async_copy(g_hbm, graw, local.at[1])]
    loads += [pltpu.make_async_copy(q_hbm.at[h], q.at[:, pl.ds(h * tok, tok)], local.at[2 + h]) for h in range(heads)]
    for load in loads:
        load.start()

    def remote(src, dst, send, recv, dev):
        return pltpu.make_async_remote_copy(
            src_ref=src, dst_ref=dst, send_sem=send, recv_sem=recv, device_id=dev, device_id_type=MESH
        )

    sent = []

    def go(copy):
        copy.start()
        sent.append(copy)

    def g_z(k, step):
        src = kwin.at[k - step, pl.ds(mine, piece)]
        return remote(src, kwin.at[k, pl.ds(mine, piece)], gz_s.at[k - 1], gz_r.at[k - 1], (ctx(step), hd))

    def g_x(n, j):
        ref = kwin.at[pl.ds(*GROUPS[n]), pl.ds(mine, piece)]
        at = n * (nhead - 1) + j - 1
        peer = lax.rem(hd + j, nhead) if n in DIRECT else xpeer(j) * 2 + c
        return remote(ref, ref, gx_s.at[at], gx_r.at[at], (s, peer))

    def g_c(n):
        ref = kwin.at[pl.ds(*GROUPS[n]), pl.ds(pl.multiple_of(c * half, 16), half)]
        return remote(ref, ref, gc_s.at[n], gc_r.at[n], (s, x * 2 + 1 - c))

    start = doc_ref[pl.ds(s, 1), :] - (s - span) * tok

    def scores(k, count):
        height = count * tok
        width = SC_HEADS * tok
        starts = jnp.concatenate([start] * SC_HEADS, axis=1)
        keys = kwin[k : k + count].reshape(height, lat)
        row = lax.broadcasted_iota(jnp.int32, (height, width), 0)
        place = row + (span - k) * tok
        if count == 2:
            place = jnp.where(row < tok, place, place - 2 * tok)
        seen = place >= starts
        if k == 0:
            token = lax.broadcasted_iota(jnp.int32, (height, tok), 1)
            seen = seen & (row <= jnp.concatenate([token] * SC_HEADS, axis=1))
        here = pl.ds(k * tok, height)

        def chunk(n, _):
            at = pl.ds(pl.multiple_of(n * width, width), width)
            score = jnp.dot(keys, q[:, at], preferred_element_type=jnp.float32)
            grad = lax.dot_general(keys[:, :LAT_C], g[at, :], NT, preferred_element_type=jnp.float32)
            score = jnp.where(seen, score, HIDDEN)
            top = jnp.max(score, axis=0, keepdims=True)
            if k > 0:
                before = tops[span + 2 : span + 3, at]
                top = jnp.maximum(top, before)
            expo = jnp.exp2((score - top) * exp2_scale)
            total = jnp.sum(expo, axis=0, keepdims=True)
            if k > 0:
                total = total + tops[span + 1 : span + 2, at] * jnp.exp2((before - top) * exp2_scale)
            for extra in range(count):
                tops[k + extra : k + extra + 1, at] = top
            tops[span + 1 : span + 2, at] = total
            tops[span + 2 : span + 3, at] = top
            ew[here, at] = expo
            gp[here, at] = grad
            return 0

        lax.fori_loop(0, heads // SC_HEADS, chunk, 0)

    def turn(k):
        kt[:, pl.ds(k * tok, tok)] = kwin[k].T

    loads[0].wait()
    kwin[0] = kt[:, pl.ds(0, tok)].T
    pl.semaphore_wait(barrier, len(peers))
    for k in FIRST:
        go(g_z(k, k))

    loads[1].wait()
    for n in range(LAT_C // LANES):
        at = pl.ds(n * LANES, LANES)
        gf[n] = graw[:, at].astype(jnp.float32)
        for h in range(heads):
            g[pl.ds(h * tok, tok), at] = gf[n, pl.ds(h, tok, stride=heads), :].astype(jnp.bfloat16)
    for load in loads[2:]:
        load.wait()
    scores(0, 1)

    def spread(n):
        for j in range(1, nhead if n in DIRECT else nx):
            go(g_x(n, j))

    def across(n):
        for j in range(1, nhead if n in DIRECT else nx):
            g_x(n, j).wait_recv()
        if n not in DIRECT:
            go(g_c(n))

    def take(n):
        if n not in DIRECT:
            g_c(n).wait_recv()
        k, count = GROUPS[n]
        scores(k, count)
        for extra in range(count):
            turn(k + extra)

    def arrive(k):
        step = FROM[k]
        g_z(k, step).wait_recv()
        for later in RELAYED.get(k, ()):
            go(g_z(later, later - k))

    def send(k):
        go(g_z(k, k))

    steps = {"send": send, "arrive": arrive, "spread": spread, "across": across, "take": take}
    for op, n in GATHER:
        steps[op](n)

    def soften(n, _):
        width = SOFT_HEADS * tok
        at = pl.ds(pl.multiple_of(n * width, width), width)
        over = 1.0 / tops[span + 1 : span + 2, at]
        final = tops[span + 2 : span + 3, at]
        delta = jnp.zeros((1, width), jnp.float32)
        for k in range(span + 1):
            here = pl.ds(k * tok, tok)
            weight = ew[here, at] * (jnp.exp2((tops[k : k + 1, at] - final) * exp2_scale) * over)
            prob = weight.astype(jnp.bfloat16)
            pw[here, at] = prob
            ew[here, at] = weight
            delta = delta + jnp.sum(prob.astype(jnp.float32) * gp[here, at], axis=0, keepdims=True)
        for k in range(span + 1):
            here = pl.ds(k * tok, tok)
            ds[here, at] = (ew[here, at] * (gp[here, at] - delta) * score_scale).astype(jnp.bfloat16)
        return 0

    lax.fori_loop(0, heads // SOFT_HEADS, soften, 0)

    def r_c(n):
        at = pl.ds(*BACK[n])
        return remote(csend.at[at], crecv.at[at], rc_s.at[n], rc_r.at[n], (s, x * 2 + 1 - c))

    def r_x(n, j):
        src = xsend.at[pl.ds(*BACK[n]), pl.ds(pl.multiple_of(xpeer(j) * piece, 16), piece)]
        dst = xrecv.at[j - 1, pl.ds(*BACK[n])]
        at = n * (nx - 1) + j - 1
        return remote(src, dst, rx_s.at[at], rx_r.at[at], (s, xpeer(j) * 2 + c))

    def r_z(k, step):
        return remote(zsend.at[k - 1], zrecv.at[k - 1], rz_s.at[k - 1], rz_r.at[k - 1], (ctx(-step), hd))

    def products(n):
        k, count = BACK[n]
        here = pl.ds(k * tok, count * tok)
        low, high = pl.multiple_of(c * half, 16), pl.multiple_of((1 - c) * half, 16)
        part[here, :] = lax.dot_general(ds[here, :], q[...], NT, preferred_element_type=jnp.float32)
        part[here, :LAT_C] += jnp.dot(pw[here, :], g[...], preferred_element_type=jnp.float32)
        for e in range(k, k + count):
            csend[e] = part[pl.ds(pl.multiple_of(e * tok + high, 16), half), :].astype(jnp.bfloat16)
        go(r_c(n))

    def pair(n):
        r_c(n).wait_recv()
        k, count = BACK[n]
        for e in range(k, k + count):
            at = pl.ds(pl.multiple_of(e * tok + c * half, 16), half)
            total = part[at, :] + crecv[e].astype(jnp.float32)
            part[at, :] = total
            xsend[e] = total.astype(jnp.bfloat16)
        for j in range(1, nx):
            go(r_x(n, j))

    def chips(n):
        for j in range(1, nx):
            r_x(n, j).wait_recv()

    def mine_of(k):
        total = part[pl.ds(pl.multiple_of(k * tok + mine, 16), piece), :]
        for j in range(1, nx):
            total = total + xrecv[j - 1, k].astype(jnp.float32)
        return total

    def leaf(k, step):
        zsend[k - 1] = mine_of(k).astype(jnp.bfloat16)
        go(r_z(k, step))

    def node(k):
        total = mine_of(k)
        for later in RELAYED[k]:
            r_z(later, later - k).wait_recv()
            total = total + zrecv[later - 1].astype(jnp.float32)
        zsend[k - 1] = total.astype(jnp.bfloat16)
        go(r_z(k, k))

    outs = []

    def queries(n):
        width = Q_HEADS * tok
        at = pl.ds(n * width, width)
        gqbuf[:, at] = jnp.dot(kt[...], ds[:, at], preferred_element_type=jnp.float32).astype(jnp.bfloat16)
        for h in range(n * Q_HEADS, (n + 1) * Q_HEADS):
            out = pltpu.make_async_copy(gqbuf.at[:, pl.ds(h * tok, tok)], gq_hbm.at[h], local.at[2 + h])
            out.start()
            outs.append(out)

    def ag(j):
        ref = glbuf.at[pl.ds(mine, piece)]
        return remote(ref, ref, ag_s.at[j - 1], ag_r.at[j - 1], (s, lax.rem(hd + j, nhead)))

    def leaves(k):
        leaf(k + 1, 2)
        leaf(k, 1)

    steps = {"products": products, "pair": pair, "chips": chips, "leaves": leaves, "node": node, "queries": queries}
    for op, n in RETURN:
        steps[op](n)

    total = mine_of(0)
    for k in reversed(STRAIGHT):
        r_z(k, k).wait_recv()
        total = total + zrecv[k - 1].astype(jnp.float32)
    glbuf[pl.ds(mine, piece), :] = total.astype(jnp.bfloat16)
    for j in range(1, nhead):
        go(ag(j))
    for out in outs:
        out.wait()
    for j in range(1, nhead):
        ag(j).wait_recv()
    glturn[...] = glbuf[...].T
    last = pltpu.make_async_copy(glturn, gl_hbm, local.at[0])
    last.start()
    for copy in sent:
        copy.wait_send()
    last.wait()


def on_device(nctx, nhead, span, queries, latents, grad_out, doc_ids):
    tok, heads, lat = queries.shape
    rows = tok * heads
    window = (span + 1) * tok
    piece, nx = tok // nhead, nhead // 2
    bf16, f32 = jnp.bfloat16, jnp.float32
    dma = pltpu.SemaphoreType.DMA
    groups, back = len(GROUPS), len(BACK)
    grad_queries, grad_latents = pl.pallas_call(
        functools.partial(kernel, span, nctx, nhead),
        out_shape=(
            jax.ShapeDtypeStruct((heads, lat, tok), bf16),
            jax.ShapeDtypeStruct((lat, tok), bf16),
        ),
        in_specs=[pl.BlockSpec(memory_space=pltpu.VMEM)] + [pl.BlockSpec(memory_space=pltpu.HBM)] * 3,
        out_specs=(pl.BlockSpec(memory_space=pltpu.HBM), pl.BlockSpec(memory_space=pl.ANY)),
        scratch_shapes=[
            pltpu.VMEM((span + 1, tok, lat), bf16),
            pltpu.VMEM((lat, window), bf16),
            pltpu.VMEM((lat, rows), bf16),
            pltpu.VMEM((rows, LAT_C), bf16),
            pltpu.VMEM((LAT_C // LANES, rows, LANES), f32),
            pltpu.VMEM((rows, LAT_C), bf16),
            pltpu.VMEM((window, rows), f32),
            pltpu.VMEM((window, rows), f32),
            pltpu.VMEM((window, rows), bf16),
            pltpu.VMEM((window, rows), bf16),
            pltpu.VMEM((span + 3, rows), f32),
            pltpu.VMEM((window, lat), f32),
            pltpu.VMEM((span + 1, tok // 2, lat), bf16),
            pltpu.VMEM((span + 1, tok // 2, lat), bf16),
            pltpu.VMEM((span + 1, tok // 2, lat), bf16),
            pltpu.VMEM((nx - 1, span + 1, piece, lat), bf16),
            pltpu.VMEM((span, piece, lat), bf16),
            pltpu.VMEM((span, piece, lat), bf16),
            pltpu.VMEM((lat, rows), bf16),
            pltpu.VMEM((tok, lat), bf16),
            pltpu.VMEM((lat, tok), bf16),
            dma((2 + heads,)),
            dma((span,)), dma((span,)),
            dma((groups * (nhead - 1),)), dma((groups * (nhead - 1),)),
            dma((groups,)), dma((groups,)),
            dma((back,)), dma((back,)),
            dma((back * (nx - 1),)), dma((back * (nx - 1),)),
            dma((span,)), dma((span,)),
            dma((nhead - 1,)), dma((nhead - 1,)),
        ],
        compiler_params=pltpu.CompilerParams(
            collective_id=0, has_side_effects=True, vmem_limit_bytes=56 * 1024 * 1024
        ),
    )(doc_ids.reshape(nctx, tok), queries.transpose(1, 2, 0), grad_out.reshape(rows, LAT_C), latents.T)
    return grad_queries.transpose(2, 0, 1), grad_latents.T


def solution(mesh):
    nctx, nhead = mesh.shape["ctx"], mesh.shape["head"]
    placed = (P("ctx", "head", None), P("ctx", None), P("ctx", "head", None), P())
    return jax.shard_map(
        functools.partial(on_device, nctx, nhead, SPAN),
        mesh=mesh,
        in_specs=placed,
        out_specs=(P("ctx", "head", None), P("ctx", None)),
        check_vma=False,
    )
```

```python
import functools

import jax
import jax.numpy as jnp
from jax import lax
from jax.experimental import pallas as pl
from jax.experimental.pallas import tpu as pltpu
from jax.sharding import PartitionSpec as P

LAT_C = 512
SPAN = 8
LANES = 128
SC_HEADS = 8
SOFT_HEADS = 2
Q_HEADS = 2

score_scale = 192.0 ** (-0.5)
exp2_scale = score_scale * 1.4426950408889634
HIDDEN = -1e30
MESH = pl.DeviceIdType.MESH
NT = (((1,), (1,)), ((), ()))

STRAIGHT = (6, 3, 2, 1)
FROM = {1: 1, 2: 2, 3: 3, 6: 6, 4: 1, 5: 2, 7: 1, 8: 2}
FIRST = (6, 3, 2, 1)
DIRECT = ()
GATHER = (
    ("arrive", 3), ("arrive", 1), ("arrive", 2), ("spread", 0), ("spread", 1), ("arrive", 6), ("spread", 2), ("across", 0),
    ("across", 1), ("arrive", 4), ("arrive", 5), ("spread", 3), ("across", 2), ("take", 0), ("arrive", 7), ("arrive", 8),
    ("spread", 4), ("take", 1), ("across", 3), ("take", 2), ("across", 4), ("take", 3), ("take", 4),
)
RELAYED = {3: (5, 4), 6: (8, 7)}
GROUPS = ((1, 2), (3, 1), (6, 1), (4, 2), (7, 2))
BACK = ((7, 2), (4, 2), (6, 1), (3, 1), (1, 2), (0, 1))
RETURN = (
    ("products", 0), ("products", 1), ("pair", 0), ("products", 2), ("pair", 1), ("products", 3), ("pair", 2),
    ("products", 4), ("chips", 0), ("leaves", 7), ("pair", 3), ("products", 5), ("pair", 4), ("chips", 1), ("leaves", 4),
    ("pair", 5), ("chips", 2), ("node", 6), ("chips", 3), ("node", 3), ("chips", 4), ("leaves", 1),
    ("queries", 0), ("queries", 1), ("queries", 2), ("queries", 3), ("chips", 5),
)


def kernel(
    span, nctx, nhead,
    doc_ref, q_hbm, g_hbm, lat_hbm, gq_hbm, gl_hbm,
    kwin, kt, q, graw, gf, g, ew, gp, pw, ds, tops, part, csend, crecv, xsend, xrecv, zsend, zrecv, gqbuf, glbuf, glturn,
    local, gz_s, gz_r, gx_s, gx_r, gc_s, gc_r, rc_s, rc_r, rx_s, rx_r, rz_s, rz_r, ag_s, ag_r,
):
    heads, lat, tok = q_hbm.shape
    rows = heads * tok
    half, piece, nx = tok // 2, tok // nhead, nhead // 2
    s = lax.axis_index("ctx")
    hd = lax.axis_index("head")
    x, c = hd // 2, lax.rem(hd, 2)
    mine = pl.multiple_of(c * half + x * piece, 16)

    def xpeer(j):
        return lax.rem(x + j, nx)

    def ctx(step):
        return lax.rem(s + step + nctx, nctx)

    barrier = pltpu.get_barrier_semaphore()
    peers = [(s, lax.rem(hd + j, nhead)) for j in range(1, nhead)]
    for step in STRAIGHT:
        peers += [(ctx(step), hd), (ctx(-step), hd)]
    for peer in peers:
        pl.semaphore_signal(barrier, inc=1, device_id=peer, device_id_type=MESH)

    loads = [pltpu.make_async_copy(lat_hbm, kt.at[:, pl.ds(0, tok)], local.at[0])]
    loads += [pltpu.make_async_copy(g_hbm, graw, local.at[1])]
    loads += [pltpu.make_async_copy(q_hbm.at[h], q.at[:, pl.ds(h * tok, tok)], local.at[2 + h]) for h in range(heads)]
    for load in loads:
        load.start()

    def remote(src, dst, send, recv, dev):
        return pltpu.make_async_remote_copy(
            src_ref=src, dst_ref=dst, send_sem=send, recv_sem=recv, device_id=dev, device_id_type=MESH
        )

    sent = []

    def go(copy):
        copy.start()
        sent.append(copy)

    def g_z(k, step):
        src = kwin.at[k - step, pl.ds(mine, piece)]
        return remote(src, kwin.at[k, pl.ds(mine, piece)], gz_s.at[k - 1], gz_r.at[k - 1], (ctx(step), hd))

    def g_x(n, j):
        ref = kwin.at[pl.ds(*GROUPS[n]), pl.ds(mine, piece)]
        at = n * (nhead - 1) + j - 1
        peer = lax.rem(hd + j, nhead) if n in DIRECT else xpeer(j) * 2 + c
        return remote(ref, ref, gx_s.at[at], gx_r.at[at], (s, peer))

    def g_c(n):
        ref = kwin.at[pl.ds(*GROUPS[n]), pl.ds(pl.multiple_of(c * half, 16), half)]
        return remote(ref, ref, gc_s.at[n], gc_r.at[n], (s, x * 2 + 1 - c))

    start = doc_ref[pl.ds(s, 1), :] - (s - span) * tok

    def scores(k, count):
        height = count * tok
        width = SC_HEADS * tok
        starts = jnp.concatenate([start] * SC_HEADS, axis=1)
        keys = kwin[k : k + count].reshape(height, lat)
        row = lax.broadcasted_iota(jnp.int32, (height, width), 0)
        place = row + (span - k) * tok
        if count == 2:
            place = jnp.where(row < tok, place, place - 2 * tok)
        seen = place >= starts
        if k == 0:
            token = lax.broadcasted_iota(jnp.int32, (height, tok), 1)
            seen = seen & (row <= jnp.concatenate([token] * SC_HEADS, axis=1))
        here = pl.ds(k * tok, height)

        def chunk(n, _):
            at = pl.ds(pl.multiple_of(n * width, width), width)
            score = jnp.dot(keys, q[:, at], preferred_element_type=jnp.float32)
            grad = lax.dot_general(keys[:, :LAT_C], g[at, :], NT, preferred_element_type=jnp.float32)
            score = jnp.where(seen, score, HIDDEN)
            top = jnp.max(score, axis=0, keepdims=True)
            if k > 0:
                before = tops[span + 2 : span + 3, at]
                top = jnp.maximum(top, before)
            expo = jnp.exp2((score - top) * exp2_scale)
            total = jnp.sum(expo, axis=0, keepdims=True)
            if k > 0:
                total = total + tops[span + 1 : span + 2, at] * jnp.exp2((before - top) * exp2_scale)
            for extra in range(count):
                tops[k + extra : k + extra + 1, at] = top
            tops[span + 1 : span + 2, at] = total
            tops[span + 2 : span + 3, at] = top
            ew[here, at] = expo
            gp[here, at] = grad
            return 0

        lax.fori_loop(0, heads // SC_HEADS, chunk, 0)

    def turn(k):
        kt[:, pl.ds(k * tok, tok)] = kwin[k].T

    loads[0].wait()
    kwin[0] = kt[:, pl.ds(0, tok)].T
    pl.semaphore_wait(barrier, len(peers))
    for k in FIRST:
        go(g_z(k, k))

    loads[1].wait()
    for n in range(LAT_C // LANES):
        at = pl.ds(n * LANES, LANES)
        gf[n] = graw[:, at].astype(jnp.float32)
        for h in range(heads):
            g[pl.ds(h * tok, tok), at] = gf[n, pl.ds(h, tok, stride=heads), :].astype(jnp.bfloat16)
    for load in loads[2:]:
        load.wait()
    scores(0, 1)

    def spread(n):
        for j in range(1, nhead if n in DIRECT else nx):
            go(g_x(n, j))

    def across(n):
        for j in range(1, nhead if n in DIRECT else nx):
            g_x(n, j).wait_recv()
        if n not in DIRECT:
            go(g_c(n))

    def take(n):
        if n not in DIRECT:
            g_c(n).wait_recv()
        k, count = GROUPS[n]
        scores(k, count)
        for extra in range(count):
            turn(k + extra)

    def arrive(k):
        step = FROM[k]
        g_z(k, step).wait_recv()
        for later in RELAYED.get(k, ()):
            go(g_z(later, later - k))

    def send(k):
        go(g_z(k, k))

    steps = {"send": send, "arrive": arrive, "spread": spread, "across": across, "take": take}
    for op, n in GATHER:
        steps[op](n)

    def soften(n, _):
        width = SOFT_HEADS * tok
        at = pl.ds(pl.multiple_of(n * width, width), width)
        over = 1.0 / tops[span + 1 : span + 2, at]
        final = tops[span + 2 : span + 3, at]
        delta = jnp.zeros((1, width), jnp.float32)
        for k in range(span + 1):
            here = pl.ds(k * tok, tok)
            weight = ew[here, at] * (jnp.exp2((tops[k : k + 1, at] - final) * exp2_scale) * over)
            prob = weight.astype(jnp.bfloat16)
            pw[here, at] = prob
            ew[here, at] = weight
            delta = delta + jnp.sum(prob.astype(jnp.float32) * gp[here, at], axis=0, keepdims=True)
        for k in range(span + 1):
            here = pl.ds(k * tok, tok)
            ds[here, at] = (ew[here, at] * (gp[here, at] - delta) * score_scale).astype(jnp.bfloat16)
        return 0

    lax.fori_loop(0, heads // SOFT_HEADS, soften, 0)

    def r_c(n):
        at = pl.ds(*BACK[n])
        return remote(csend.at[at], crecv.at[at], rc_s.at[n], rc_r.at[n], (s, x * 2 + 1 - c))

    def r_x(n, j):
        src = xsend.at[pl.ds(*BACK[n]), pl.ds(pl.multiple_of(xpeer(j) * piece, 16), piece)]
        dst = xrecv.at[j - 1, pl.ds(*BACK[n])]
        at = n * (nx - 1) + j - 1
        return remote(src, dst, rx_s.at[at], rx_r.at[at], (s, xpeer(j) * 2 + c))

    def r_z(k, step):
        return remote(zsend.at[k - 1], zrecv.at[k - 1], rz_s.at[k - 1], rz_r.at[k - 1], (ctx(-step), hd))

    def products(n):
        k, count = BACK[n]
        here = pl.ds(k * tok, count * tok)
        low, high = pl.multiple_of(c * half, 16), pl.multiple_of((1 - c) * half, 16)
        part[here, :] = lax.dot_general(ds[here, :], q[...], NT, preferred_element_type=jnp.float32)
        part[here, :LAT_C] += jnp.dot(pw[here, :], g[...], preferred_element_type=jnp.float32)
        for e in range(k, k + count):
            csend[e] = part[pl.ds(pl.multiple_of(e * tok + high, 16), half), :].astype(jnp.bfloat16)
        go(r_c(n))

    def pair(n):
        r_c(n).wait_recv()
        k, count = BACK[n]
        for e in range(k, k + count):
            at = pl.ds(pl.multiple_of(e * tok + c * half, 16), half)
            total = part[at, :] + crecv[e].astype(jnp.float32)
            part[at, :] = total
            xsend[e] = total.astype(jnp.bfloat16)
        for j in range(1, nx):
            go(r_x(n, j))

    def chips(n):
        for j in range(1, nx):
            r_x(n, j).wait_recv()

    def mine_of(k):
        total = part[pl.ds(pl.multiple_of(k * tok + mine, 16), piece), :]
        for j in range(1, nx):
            total = total + xrecv[j - 1, k].astype(jnp.float32)
        return total

    def leaf(k, step):
        zsend[k - 1] = mine_of(k).astype(jnp.bfloat16)
        go(r_z(k, step))

    def node(k):
        total = mine_of(k)
        for later in RELAYED[k]:
            r_z(later, later - k).wait_recv()
            total = total + zrecv[later - 1].astype(jnp.float32)
        zsend[k - 1] = total.astype(jnp.bfloat16)
        go(r_z(k, k))

    outs = []

    def queries(n):
        width = Q_HEADS * tok
        at = pl.ds(n * width, width)
        gqbuf[:, at] = jnp.dot(kt[...], ds[:, at], preferred_element_type=jnp.float32).astype(jnp.bfloat16)
        for h in range(n * Q_HEADS, (n + 1) * Q_HEADS):
            out = pltpu.make_async_copy(gqbuf.at[:, pl.ds(h * tok, tok)], gq_hbm.at[h], local.at[2 + h])
            out.start()
            outs.append(out)

    def ag(j):
        ref = glbuf.at[pl.ds(mine, piece)]
        return remote(ref, ref, ag_s.at[j - 1], ag_r.at[j - 1], (s, lax.rem(hd + j, nhead)))

    def leaves(k):
        leaf(k + 1, 2)
        leaf(k, 1)

    steps = {"products": products, "pair": pair, "chips": chips, "leaves": leaves, "node": node, "queries": queries}
    for op, n in RETURN:
        steps[op](n)

    total = mine_of(0)
    for k in reversed(STRAIGHT):
        r_z(k, k).wait_recv()
        total = total + zrecv[k - 1].astype(jnp.float32)
    glbuf[pl.ds(mine, piece), :] = total.astype(jnp.bfloat16)
    for j in range(1, nhead):
        go(ag(j))
    for out in outs:
        out.wait()
    for j in range(1, nhead):
        ag(j).wait_recv()
    glturn[...] = glbuf[...].T
    last = pltpu.make_async_copy(glturn, gl_hbm, local.at[0])
    last.start()
    for copy in sent:
        copy.wait_send()
    last.wait()


def on_device(nctx, nhead, span, queries, latents, grad_out, doc_ids):
    tok, heads, lat = queries.shape
    rows = tok * heads
    window = (span + 1) * tok
    piece, nx = tok // nhead, nhead // 2
    bf16, f32 = jnp.bfloat16, jnp.float32
    dma = pltpu.SemaphoreType.DMA
    groups, back = len(GROUPS), len(BACK)
    grad_queries, grad_latents = pl.pallas_call(
        functools.partial(kernel, span, nctx, nhead),
        out_shape=(
            jax.ShapeDtypeStruct((heads, lat, tok), bf16),
            jax.ShapeDtypeStruct((lat, tok), bf16),
        ),
        in_specs=[pl.BlockSpec(memory_space=pltpu.VMEM)] + [pl.BlockSpec(memory_space=pltpu.HBM)] * 3,
        out_specs=(pl.BlockSpec(memory_space=pltpu.HBM), pl.BlockSpec(memory_space=pl.ANY)),
        scratch_shapes=[
            pltpu.VMEM((span + 1, tok, lat), bf16),
            pltpu.VMEM((lat, window), bf16),
            pltpu.VMEM((lat, rows), bf16),
            pltpu.VMEM((rows, LAT_C), bf16),
            pltpu.VMEM((LAT_C // LANES, rows, LANES), f32),
            pltpu.VMEM((rows, LAT_C), bf16),
            pltpu.VMEM((window, rows), f32),
            pltpu.VMEM((window, rows), f32),
            pltpu.VMEM((window, rows), bf16),
            pltpu.VMEM((window, rows), bf16),
            pltpu.VMEM((span + 3, rows), f32),
            pltpu.VMEM((window, lat), f32),
            pltpu.VMEM((span + 1, tok // 2, lat), bf16),
            pltpu.VMEM((span + 1, tok // 2, lat), bf16),
            pltpu.VMEM((span + 1, tok // 2, lat), bf16),
            pltpu.VMEM((nx - 1, span + 1, piece, lat), bf16),
            pltpu.VMEM((span, piece, lat), bf16),
            pltpu.VMEM((span, piece, lat), bf16),
            pltpu.VMEM((lat, rows), bf16),
            pltpu.VMEM((tok, lat), bf16),
            pltpu.VMEM((lat, tok), bf16),
            dma((2 + heads,)),
            dma((span,)), dma((span,)),
            dma((groups * (nhead - 1),)), dma((groups * (nhead - 1),)),
            dma((groups,)), dma((groups,)),
            dma((back,)), dma((back,)),
            dma((back * (nx - 1),)), dma((back * (nx - 1),)),
            dma((span,)), dma((span,)),
            dma((nhead - 1,)), dma((nhead - 1,)),
        ],
        compiler_params=pltpu.CompilerParams(
            collective_id=0, has_side_effects=True, vmem_limit_bytes=56 * 1024 * 1024
        ),
    )(doc_ids.reshape(nctx, tok), queries.transpose(1, 2, 0), grad_out.reshape(rows, LAT_C), latents.T)
    return grad_queries.transpose(2, 0, 1), grad_latents.T


def solution(mesh):
    nctx, nhead = mesh.shape["ctx"], mesh.shape["head"]
    placed = (P("ctx", "head", None), P("ctx", None), P("ctx", "head", None), P())
    return jax.shard_map(
        functools.partial(on_device, nctx, nhead, SPAN),
        mesh=mesh,
        in_specs=placed,
        out_specs=(P("ctx", "head", None), P("ctx", None)),
        check_vma=False,
    )
```
